512 devices in a mesh: seq: 64 (over z, y), head: 8 (over x, core).
Axes of the slice: x: 4, y: 8, z: 8, core: 2. Of those that a mesh axis runs over, the one named last changes fastest.
Arguments:
- queries: bfloat16 [8192, 2048], P('seq', 'head'), may hold values from -6 to 6
- key_vectors: bfloat16 [2, 8192, 2048], P(None, 'seq', 'head'), may hold values from -6 to 6
- values: bfloat16 [2, 8192, 2048], P(None, 'seq', 'head'), may hold values from -6 to 6
- strengths: float32 [2, 16, 8192], P(None, 'head', 'seq'), may hold values from 0.05 to 1.95
- out_weight: bfloat16 [2048, 4096], P('head', 'seq'), may hold values from -0.375 to 0.375
Outputs:
- mixed: bfloat16 [8192, 4096], P('seq', 'head')
The draws below stay inside these ranges and needn't reach their ends.
All inputs are finite; a program needn't handle non-finite values.
Results may differ from the reference program's by a relative error of at most 0.014.
Values may be sent and summed in bfloat16 or wider, within the bound.
A program may use at most 64 MiB of HBM per device.

```python
import jax
import jax.numpy as jnp
from jax import lax

D = 4096
H = 16
DK = 128
BLOCK = 64
TOKENS = 8192
N_HEAD = 8


def draw_key_vectors(key, part):
    base_key, head_key, dim_key, scale_key = jax.random.split(jax.random.fold_in(key, 7), 4)
    base = jnp.clip(jax.random.normal(base_key, (2, TOKENS, H, DK), jnp.float32), -6.0, 6.0)
    slow_head = jax.random.randint(head_key, (H,), 0, 2) > 0
    weak_dim = jax.random.randint(dim_key, (H, DK), 0, 4) > 0
    block_scale = jnp.exp(jax.random.uniform(scale_key, (TOKENS // BLOCK, 1, H, 1), jnp.float32, jnp.log(0.01), jnp.log(0.04)))
    block_scale = jnp.repeat(block_scale, BLOCK, axis=0)[:, 0]
    factor = jnp.where((slow_head[:, None] & weak_dim)[None], block_scale, 1.0)
    return (base * factor[None]).reshape(2, TOKENS, H * DK).astype(jnp.bfloat16)


def raised(drawn, own_key, source, target, parts, factor):
    owner, partner = [(jnp.arange(drawn.shape[position]) // (drawn.shape[position] // parts)).reshape([-1 if axis == position else 1 for axis in range(drawn.ndim)]) for position in (source, target)]
    chosen = jax.random.permutation(own_key, parts)[partner]
    strong = (owner == chosen) | (owner == (partner + parts // 2) % parts)
    return jnp.where(strong, factor * drawn, drawn)


def level_of(stream_key, dims, pieces, low, high):
    gain = 1.0
    for position, shards_of in pieces:
        heights = jax.random.uniform(jax.random.fold_in(jax.random.fold_in(stream_key, 6), position), (shards_of,), jnp.float32, low / len(pieces), high / len(pieces))
        gain = gain * jnp.repeat(jnp.exp(heights), dims[position] // shards_of).reshape((-1,) + (1,) * (len(dims) - 1 - position))
    return gain


def gaussian(stream_key, extent, scale, bound, cuts=(), held_as=jnp.bfloat16):
    result = scale * jax.random.normal(stream_key, extent, jnp.float32)
    if cuts:
        result = result * level_of(stream_key, extent, cuts, -0.22, 0.18)
    return jnp.clip(result, -bound, bound).astype(held_as)


def heavy_noise(key, dims, width, reach, pieces, heavy, kind=jnp.bfloat16):
    drawn = width * jax.random.normal(key, dims, jnp.float32)
    if pieces:
        drawn = drawn * level_of(key, dims, pieces, -0.22, 0.18)
    return jnp.clip(raised(drawn, jax.random.fold_in(key, 3), *heavy), -reach, reach).astype(kind)


def setup_inputs(seed: int = 0) -> dict:
    key_of = jax.random.split(jax.random.key(seed), 6)
    queries = gaussian(key_of[0], (TOKENS, H * DK), 1.0, 6.0, ((0, 64), (1, 8)))
    key_vectors = draw_key_vectors(jax.random.fold_in(key_of[5], 71), 0)
    values = gaussian(key_of[2], (2, TOKENS, H * DK), 1.0, 6.0, ((1, 64), (2, 8)))
    strengths = jnp.clip(0.05 + 1.90000005 * jax.random.uniform(key_of[3], (2, H, TOKENS), jnp.float32) ** level_of(key_of[3], (2, H, TOKENS), ((1, 8), (2, 64)), -0.2, 0.2), 0.05, 1.95)
    out_weight = heavy_noise(key_of[4], (H * DK, D), (H * DK) ** -0.5, 0.375, ((0, 8), (1, 64)), (0, 1, 64, 4.0))
    return dict(queries=queries, key_vectors=key_vectors, values=values, strengths=strengths, out_weight=out_weight)


HIGHEST_PRECISION = lax.Precision.HIGHEST

def unit_rows(matrix):
    return matrix * lax.rsqrt(lax.optimization_barrier(jnp.sum(matrix * matrix, axis=-1, keepdims=True)) + 1e-06)

def reflect_block(state, block):
    query_block, key_block, value_block, beta_block = block
    head_count = beta_block.shape[1]
    rows = query_block.shape[0]
    head_width = query_block.shape[1] // head_count
    query_heads = jnp.transpose(unit_rows(query_block.astype(jnp.float32).reshape(rows, head_count, head_width)), (1, 0, 2))
    key_heads = jnp.transpose(unit_rows(key_block.astype(jnp.float32).reshape(2, rows, head_count, head_width)), (2, 1, 0, 3)).reshape(head_count, 2 * rows, head_width)
    value_heads = jnp.transpose(value_block.astype(jnp.float32).reshape(2, rows, head_count, head_width), (2, 1, 0, 3)).reshape(head_count, 2 * rows, head_width)
    beta_heads = jnp.transpose(beta_block, (1, 2, 0)).reshape(head_count, 2 * rows)
    key_gram = jnp.einsum('hik,hjk->hij', key_heads, key_heads, precision=HIGHEST_PRECISION)
    system = jnp.tril(key_gram, -1) * beta_heads[:, :, None] + jnp.eye(2 * rows, dtype=jnp.float32)
    right_side = beta_heads[:, :, None] * (value_heads - jnp.einsum('hik,hvk->hiv', key_heads, state, precision=HIGHEST_PRECISION))
    updates = jax.scipy.linalg.solve_triangular(system, right_side, lower=True, unit_diagonal=True)
    row_ids = lax.broadcasted_iota(jnp.int32, (rows, 2 * rows), 0)
    col_ids = lax.broadcasted_iota(jnp.int32, (rows, 2 * rows), 1)
    reach_mask = (col_ids <= 2 * row_ids + 1).astype(jnp.float32)
    scores = jnp.einsum('htk,hik->hti', query_heads, key_heads, precision=HIGHEST_PRECISION) * reach_mask
    block_out = jnp.einsum('hvk,htk->htv', state, query_heads, precision=HIGHEST_PRECISION) + jnp.einsum('hti,hiv->htv', scores, updates, precision=HIGHEST_PRECISION)
    new_state = state + jnp.einsum('hiv,hik->hvk', updates, key_heads, precision=HIGHEST_PRECISION)
    return (new_state, block_out)

def reference(queries, key_vectors, values, strengths, out_weight):
    block_count = TOKENS // BLOCK
    query_blocks = queries.reshape(block_count, BLOCK, H * DK)
    key_blocks = jnp.moveaxis(key_vectors.reshape(2, block_count, BLOCK, H * DK), 1, 0)
    value_blocks = jnp.moveaxis(values.reshape(2, block_count, BLOCK, H * DK), 1, 0)
    beta_blocks = jnp.moveaxis(strengths.reshape(2, H, block_count, BLOCK), 2, 0)
    initial = jnp.zeros((H, DK, DK), jnp.float32)
    final_state, outputs = lax.scan(reflect_block, initial, (query_blocks, key_blocks, value_blocks, beta_blocks))
    heads_out = jnp.transpose(outputs, (0, 2, 1, 3)).reshape(TOKENS, H * DK).astype(jnp.bfloat16)
    group_rows = H * DK // N_HEAD
    total = jnp.zeros((TOKENS, D), jnp.float32)
    for group in range(N_HEAD):
        lower_row = group * group_rows
        upper_row = lower_row + group_rows
        group_sum = jnp.dot(heads_out[:, lower_row:upper_row].astype(jnp.float32), out_weight[lower_row:upper_row].astype(jnp.float32), preferred_element_type=jnp.float32)
        total = total + group_sum.astype(jnp.bfloat16).astype(jnp.float32)
    return total.astype(jnp.bfloat16)
```

```python
import functools

import jax
import jax.numpy as jnp
from jax import lax
from jax.experimental import pallas as pl
from jax.experimental.pallas import tpu as pltpu
from jax.sharding import PartitionSpec as P

MESH = pl.DeviceIdType.MESH
F32 = jnp.float32
BF16 = jnp.bfloat16


def dot(a, b):
    return jnp.dot(a, b, preferred_element_type=F32)


def dot_nt(a, b):
    return lax.dot_general(a, b, (((1,), (1,)), ((), ())), preferred_element_type=F32)


def dot_tn(a, b):
    return lax.dot_general(a, b, (((0,), (0,)), ((), ())), preferred_element_type=F32)


def split(a):
    high = a.astype(BF16)
    return high, (a - high.astype(F32)).astype(BF16)


def dot3(a, b):
    return dot(a[0], b[0]) + (dot(a[1], b[0]) + dot(a[0], b[1]))


class Ring:
    def __init__(self, n, place, device_at, slot, send, recv):
        self.n, self.place, self.device_at, self.slot = n, place, device_at, slot
        self.send, self.recv = send, recv

    def parts(self, hop, way):
        return (way,) if hop == self.n // 2 - 1 else (0, 1)

    def copy(self, hop, way, part, arriving):
        n, sign = self.n, (1, -1)[way]
        owner = lax.rem(self.place + 2 * n - sign * (hop + arriving), n)
        block = self.slot(owner, part)
        return pltpu.make_async_remote_copy(
            src_ref=block,
            dst_ref=block,
            send_sem=self.send.at[way, hop, part],
            recv_sem=self.recv.at[way, hop, part],
            device_id=self.device_at(lax.rem(self.place + n + sign, n)),
            device_id_type=MESH,
        )

    def hop(self, hop):
        for part in (0, 1):
            for way in (0, 1):
                if hop > 0 and part in self.parts(hop - 1, way):
                    self.copy(hop - 1, way, part, 1).wait_recv()
                if hop < self.n // 2 and part in self.parts(hop, way):
                    self.copy(hop, way, part, 0).start()

    def finish(self):
        for hop in range(self.n // 2):
            for way in (0, 1):
                for part in self.parts(hop, way):
                    self.copy(hop, way, part, 0).wait_send()


def kernel(
    nz, ny, nh,
    q_ref, k_ref, v_ref, b_ref, w_ref, o_ref,
    k_int, v_int, wt, wa, wb, d_all, g_out, g_in, m_all, e_all, s_pre, s_out, s_in, h_all,
    wt_send, wt_recv, wa1_send, wa1_recv, wb1_send, wb1_recv, wa2_send, wa2_recv, wb2_send, wb2_recv,
    d_send, d_recv, g_send, g_recv, m_send, m_recv, s_send, s_recv, x_send, x_recv, c_send, c_recv,
):
    seq, head = lax.axis_index("seq"), lax.axis_index("head")
    z, y = seq // ny, lax.rem(seq, ny)
    x, core = head // 2, lax.rem(head, 2)
    nx = nh // 2
    heads = b_ref.shape[1]
    toks = q_ref.shape[0]
    dk = q_ref.shape[1] // heads
    refl = 2 * toks
    sl = dk // ny
    off_diagonal = z != head

    barrier = pltpu.get_barrier_semaphore()
    partners = [(z * ny + lax.rem(y + d, ny), head) for d in range(1, ny)]
    z_ring = {1, nz - 1}
    partners += [(lax.rem(z + d, nz) * ny + y, head) for d in sorted(z_ring)]
    x_ring = {1, nx - 1} - {0}
    partners += [(seq, lax.rem(x + d, nx) * 2 + core) for d in sorted(x_ring)]
    partners += [(seq, x * 2 + 1 - core)]
    for partner in partners:
        pl.semaphore_signal(barrier, inc=1, device_id=partner, device_id_type=MESH)

    @pl.when(off_diagonal)
    def _():
        pl.semaphore_signal(
            barrier, inc=1, device_id=(head * ny + y, z), device_id_type=MESH
        )

    def enter():
        pl.semaphore_wait(barrier, len(partners) + off_diagonal.astype(jnp.int32))

    def turned(half, dst):
        return pltpu.make_async_remote_copy(
            src_ref=wt.at[half],
            dst_ref=dst,
            send_sem=wt_send.at[half],
            recv_sem=wt_recv.at[half],
            device_id=(head * ny + y, z),
            device_id_type=MESH,
        )

    cols = w_ref.shape[1]
    eye_cols = (
        lax.broadcasted_iota(jnp.int32, (cols, cols), 0)
        == lax.broadcasted_iota(jnp.int32, (cols, cols), 1)
    ).astype(BF16)
    for half in (0, 1):
        wt[half] = dot_nt(eye_cols, w_ref[half * dk : (half + 1) * dk, :]).astype(BF16)

    def send_turned():
        @pl.when(off_diagonal)
        def _():
            turned(0, wa.at[head, y]).start()
            turned(1, wb.at[y, head]).start()

        @pl.when(jnp.logical_not(off_diagonal))
        def _():
            wa[z, y] = wt[0]
            wb[y, z] = wt[1]

    def take_turned():
        @pl.when(off_diagonal)
        def _():
            turned(0, wa.at[z, y]).wait_recv()
            turned(1, wb.at[y, z]).wait_recv()

    def on_y(i):
        return (z * ny + i, head)

    def on_z(i):
        return (i * ny + y, head)

    def on_x(i):
        return (seq, i * 2 + core)

    half_cols = cols // 2

    def rows(part):
        return pl.ds(part * half_cols, half_cols)

    wa1 = Ring(ny, y, on_y, lambda i, p: wa.at[z, i, rows(p)], wa1_send, wa1_recv)
    wb1 = Ring(nz, z, on_z, lambda i, p: wb.at[y, i, rows(p)], wb1_send, wb1_recv)
    wa2 = Ring(nz, z, on_z, lambda i, p: wa.at[i, pl.ds(p * (ny // 2), ny // 2)], wa2_send, wa2_recv)
    wb2 = Ring(ny, y, on_y, lambda i, p: wb.at[i, pl.ds(p * (nz // 2), nz // 2)], wb2_send, wb2_recv)
    d_ring = Ring(ny, y, on_y, lambda i, p: d_all.at[i, p], d_send, d_recv)
    m_ring = Ring(nz, z, on_z, lambda i, p: m_all.at[i, p], m_send, m_recv)
    x_rg = Ring(nx, x, on_x, lambda i, p: h_all.at[i * 2 + core, p], x_send, x_recv)

    def to_y(d, out, into, send, recv, arriving):
        peer = lax.rem(y + d, ny)
        other = lax.rem(y + ny - d, ny)
        return pltpu.make_async_remote_copy(
            src_ref=out.at[other if arriving else peer],
            dst_ref=into.at[other if arriving else y],
            send_sem=send.at[d],
            recv_sem=recv.at[d],
            device_id=on_y(peer),
            device_id_type=MESH,
        )

    enter()
    send_turned()

    tok_id = lax.broadcasted_iota(jnp.int32, (refl, toks), 1)
    row_of = lax.broadcasted_iota(jnp.int32, (refl, toks), 0)
    ri = lax.broadcasted_iota(jnp.int32, (refl, refl), 0)
    ci = lax.broadcasted_iota(jnp.int32, (refl, refl), 1)
    keys, systems, inverses, sides = [], [], [], []
    for h in range(heads):
        cut = slice(h * dk, (h + 1) * dk)
        for j in (0, 1):
            k_int[h, pl.ds(j, toks, stride=2), :] = k_ref[j, :, cut].astype(F32)
            v_int[h, pl.ds(j, toks, stride=2), :] = v_ref[j, :, cut].astype(F32)
    for h in range(heads):
        key = k_int[h]
        inv = lax.rsqrt(jnp.sum(key * key, axis=1, keepdims=True) + 1e-06)
        picked = jnp.where(
            lax.rem(row_of, 2) == 0, b_ref[0, h : h + 1, :], b_ref[1, h : h + 1, :]
        )
        beta = jnp.sum(jnp.where(row_of // 2 == tok_id, picked, 0.0), axis=1, keepdims=True)
        beta_inv = beta * inv
        gain = beta_inv * inv
        kb = key.astype(BF16)
        keys.append(kb)
        systems.append(jnp.where(ri > ci, gain * dot_nt(kb, kb), 0.0))
        sides.append(jnp.concatenate([gain * key, beta_inv * v_int[h]], axis=1))
    eye = (ri == ci).astype(F32)
    inverses = [eye - jnp.where((ri >> 1) == (ci >> 1), a, 0.0) for a in systems]
    level = 1
    background = {2: [take_turned, lambda: wa1.hop(0), lambda: wb1.hop(0)]}
    for step in range(1, ny // 2 + 1):
        background.setdefault(2 + step, []).append(functools.partial(wa1.hop, step))
    for step in range(1, nz // 2 + 1):
        background.setdefault(2 + step, []).append(functools.partial(wb1.hop, step))
    while (1 << level) < refl:
        here = ((ri >> (level + 1)) == (ci >> (level + 1))) & ((ri >> level) != (ci >> level))
        for h in range(heads):
            xb = inverses[h].astype(BF16)
            inner = dot(jnp.where(here, systems[h], 0.0).astype(BF16), xb)
            inverses[h] = inverses[h] - dot(xb, inner.astype(BF16))
        for act in background.pop(level, []):
            act()
        level += 1
    for left in sorted(background):
        for act in background[left]:
            act()
    wa2.hop(0)
    solved = []
    for h in range(heads):
        xs = split(inverses[h])
        residual = (eye - inverses[h]) - dot3(split(systems[h]), xs)
        fine = split(inverses[h] + dot(xs[0], residual.astype(BF16)))
        solved.append(dot3(fine, split(sides[h])))
    for h in range(heads):
        sh, slo = split(solved[h])
        moved = dot_tn(sh, keys[h]) + dot_tn(slo, keys[h])
        d_all[y, h] = moved[:dk].astype(BF16)
        g_out[:, h] = moved[dk:].astype(BF16).reshape(ny, sl, dk)
    d_ring.hop(0)
    for d in range(1, ny):
        to_y(d, g_out, g_in, g_send, g_recv, 0).start()
    g_in[y] = g_out[y]

    reach = (
        lax.broadcasted_iota(jnp.int32, (toks, refl), 1)
        <= 2 * lax.broadcasted_iota(jnp.int32, (toks, refl), 0) + 1
    )
    reads, locals_, q_inv = [], [], []

    def read_head(h):
        qb = q_ref[:, h * dk : (h + 1) * dk]
        qf = qb.astype(F32)
        q_inv.append(lax.rsqrt(jnp.sum(qf * qf, axis=1, keepdims=True) + 1e-06))
        scores = jnp.where(reach, dot_nt(qb, keys[h]), 0.0)
        both = dot3(split(scores), split(solved[h]))
        reads.append((qf - both[:, :dk]).astype(BF16))
        locals_.append(both[:, dk:])

    for step in range(max(heads, ny // 2)):
        if step < heads:
            read_head(step)
        if step < ny // 2:
            d_ring.hop(step + 1)
    for d in range(1, ny):
        to_y(d, g_out, g_in, g_send, g_recv, 1).wait_recv()

    top = (
        lax.broadcasted_iota(jnp.int32, (dk + sl, dk), 0)
        == lax.broadcasted_iota(jnp.int32, (dk + sl, dk), 1)
    ).astype(F32)
    stack = [jnp.zeros((dk + sl, dk), F32) for _ in range(heads)]
    pad = jnp.zeros((dk, dk), F32)
    for i in range(ny):
        for h in range(heads):
            e_all[h, :, i * dk : (i + 1) * dk] = stack[h][:dk].astype(BF16)
            s_pre[i, h] = stack[h][dk:]
            grown = jnp.concatenate([pad, g_in[i, h].astype(F32)], axis=0)
            stack[h] = stack[h] + dot((top - stack[h]).astype(BF16), d_all[i, h]) + grown
    for h in range(heads):
        m_all[z, h] = stack[h].astype(BF16)
    m_ring.hop(0)
    wa2.hop(1)
    wb2.hop(0)
    for step in range(1, nz // 2 + 1):
        m_ring.hop(step)
    state = [jnp.zeros((sl, dk), F32) for _ in range(heads)]
    for i in range(nz - 1):
        for h in range(heads):
            after = state[h] - dot(state[h].astype(BF16), m_all[i, h, :dk]) + m_all[i, h, dk:].astype(F32)
            state[h] = jnp.where(i < z, after, state[h])
    for h in range(heads):
        drop = dot(state[h].astype(BF16), e_all[h])
        for i in range(ny):
            s_out[i, h] = (state[h] - drop[:, i * dk : (i + 1) * dk] + s_pre[i, h]).astype(BF16)
    for d in range(1, ny):
        to_y(d, s_out, s_in, s_send, s_recv, 0).start()
    s_in[y] = s_out[y]
    for step in range(2, nz // 2 + 1):
        wa2.hop(step)
    for step in range(1, ny // 2 + 1):
        wb2.hop(step)
    for d in range(1, ny):
        to_y(d, s_out, s_in, s_send, s_recv, 1).wait_recv()
    for h in range(heads):
        carried = s_in[:, h].reshape(dk, dk)
        h_all[head, h] = (q_inv[h] * (dot_nt(reads[h], carried) + locals_[h])).astype(BF16)

    def across(i, h, arriving):
        block = h_all.at[i * 2 + (1 - core if arriving else core), h]
        return pltpu.make_async_remote_copy(
            src_ref=block,
            dst_ref=block,
            send_sem=c_send.at[i, h],
            recv_sem=c_recv.at[i, h],
            device_id=(seq, x * 2 + 1 - core),
            device_id_type=MESH,
        )

    if nx > 1:
        x_rg.hop(0)
        for step in range(1, nx // 2 + 1):
            x_rg.hop(step)
    for i in range(nx):
        for h in range(heads):
            across(i, h, 0).start()
    total = None
    for i in range(nx):
        for h in range(heads):
            across(i, h, 1).wait_recv()
    for i in range(nh):
        left = jnp.concatenate([h_all[i, h] for h in range(heads)], axis=1)
        right = jnp.concatenate(
            [wa[i].reshape(ny * cols, dk), wb[:, i].reshape(ny * cols, dk)], axis=1
        )
        term = dot_nt(left, right)
        total = term if total is None else total + term
    o_ref[...] = total.astype(BF16)

    @pl.when(off_diagonal)
    def _():
        turned(0, wa.at[head, y]).wait_send()
        turned(1, wb.at[y, head]).wait_send()

    for ring in (wa1, wb1, wa2, wb2, d_ring, m_ring) + ((x_rg,) if nx > 1 else ()):
        ring.finish()
    for d in range(1, ny):
        to_y(d, g_out, g_in, g_send, g_recv, 0).wait_send()
        to_y(d, s_out, s_in, s_send, s_recv, 0).wait_send()
    for i in range(nx):
        for h in range(heads):
            across(i, h, 0).wait_send()


def solution(mesh):
    nh = mesh.shape["head"]
    nz = nh
    ny = mesh.shape["seq"] // nz
    nx = nh // 2

    def per_device(queries, key_vectors, values, strengths, out_weight):
        toks = queries.shape[0]
        heads = strengths.shape[1]
        dk = queries.shape[1] // heads
        cols = out_weight.shape[1]
        sl = dk // ny
        vmem, dma = pltpu.VMEM, pltpu.SemaphoreType.DMA

        def ring(n):
            return [dma((2, max(n // 2, 1), 2))] * 2

        return pl.pallas_call(
            functools.partial(kernel, nz, ny, nh),
            out_shape=jax.ShapeDtypeStruct((toks, ny * cols), BF16),
            in_specs=[pl.BlockSpec(memory_space=pltpu.VMEM)] * 5,
            out_specs=pl.BlockSpec(memory_space=pltpu.VMEM),
            scratch_shapes=[
                vmem((heads, 2 * toks, dk), F32),
                vmem((heads, 2 * toks, dk), F32),
                vmem((2, cols, dk), BF16),
                vmem((nz, ny, cols, dk), BF16),
                vmem((ny, nz, cols, dk), BF16),
                vmem((ny, heads, dk, dk), BF16),
                vmem((ny, heads, sl, dk), BF16),
                vmem((ny, heads, sl, dk), BF16),
                vmem((nz, heads, dk + sl, dk), BF16),
                vmem((heads, dk, ny * dk), BF16),
                vmem((ny, heads, sl, dk), F32),
                vmem((ny, heads, sl, dk), BF16),
                vmem((ny, heads, sl, dk), BF16),
                vmem((nh, heads, toks, dk), BF16),
                dma((2,)),
                dma((2,)),
                *ring(ny),
                *ring(nz),
                *ring(nz),
                *ring(ny),
                *ring(ny),
                dma((ny,)),
                dma((ny,)),
                *ring(nz),
                dma((ny,)),
                dma((ny,)),
                *ring(nx),
                dma((nx, heads)),
                dma((nx, heads)),
            ],
            compiler_params=pltpu.CompilerParams(
                collective_id=0, has_side_effects=True, vmem_limit_bytes=48 * 1024 * 1024
            ),
        )(queries, key_vectors, values, strengths, out_weight)

    return jax.shard_map(
        per_device,
        mesh=mesh,
        in_specs=(
            P("seq", "head"),
            P(None, "seq", "head"),
            P(None, "seq", "head"),
            P(None, "head", "seq"),
            P("head", "seq"),
        ),
        out_specs=P("seq", "head"),
        check_vma=False,
    )
```

```python
import functools

import jax
import jax.numpy as jnp
from jax import lax
from jax.experimental import pallas as pl
from jax.experimental.pallas import tpu as pltpu
from jax.sharding import PartitionSpec as P

MESH = pl.DeviceIdType.MESH
F32 = jnp.float32
BF16 = jnp.bfloat16


def dot(a, b):
    return jnp.dot(a, b, preferred_element_type=F32)


def dot_nt(a, b):
    return lax.dot_general(a, b, (((1,), (1,)), ((), ())), preferred_element_type=F32)


def dot_tn(a, b):
    return lax.dot_general(a, b, (((0,), (0,)), ((), ())), preferred_element_type=F32)


def split(a):
    high = a.astype(BF16)
    return high, (a - high.astype(F32)).astype(BF16)


def dot3(a, b):
    return dot(a[0], b[0]) + (dot(a[1], b[0]) + dot(a[0], b[1]))


class Ring:
    def __init__(self, n, place, device_at, slot, send, recv):
        self.n, self.place, self.device_at, self.slot = n, place, device_at, slot
        self.send, self.recv = send, recv

    def parts(self, hop, way):
        return (way,) if hop == self.n // 2 - 1 else (0, 1)

    def copy(self, hop, way, part, arriving):
        n, sign = self.n, (1, -1)[way]
        owner = lax.rem(self.place + 2 * n - sign * (hop + arriving), n)
        block = self.slot(owner, part)
        return pltpu.make_async_remote_copy(
            src_ref=block,
            dst_ref=block,
            send_sem=self.send.at[way, hop, part],
            recv_sem=self.recv.at[way, hop, part],
            device_id=self.device_at(lax.rem(self.place + n + sign, n)),
            device_id_type=MESH,
        )

    def hop(self, hop):
        if hop > self.n // 2:
            return
        for part in (0, 1):
            for way in (0, 1):
                if hop > 0 and part in self.parts(hop - 1, way):
                    self.copy(hop - 1, way, part, 1).wait_recv()
                if hop < self.n // 2 and part in self.parts(hop, way):
                    self.copy(hop, way, part, 0).start()

    def finish(self):
        for hop in range(self.n // 2):
            for way in (0, 1):
                for part in self.parts(hop, way):
                    self.copy(hop, way, part, 0).wait_send()


def kernel(
    nz, ny, nh,
    q_hbm, k_hbm, v_hbm, b_hbm, w_hbm, o_ref,
    q_ref, k_ref, v_ref, b_ref, w_ref, k_int, v_int, wa, wb, pay_out, pay_in, m_out, m_in, e_all, s_pre, s_out, s_in, h_all,
    load_sem, a_send, a_recv, b_send, b_recv, wa_send, wa_recv, wb_send, wb_recv,
    d_send, d_recv, m_send, m_recv, s_send, s_recv, x_send, x_recv, c_send, c_recv,
):
    seq, head = lax.axis_index("seq"), lax.axis_index("head")
    z, y = seq // ny, lax.rem(seq, ny)
    x, core = head // 2, lax.rem(head, 2)
    nx = nh // 2
    heads = b_ref.shape[1]
    toks = q_ref.shape[0]
    dk = q_ref.shape[1] // heads
    refl = 2 * toks
    per = ny // heads
    sl = dk // per
    off_diagonal = z != head
    sibling = (seq, x * 2 + 1 - core)

    def on_y(i):
        return (z * ny + i, head)

    def on_z(i):
        return (i * ny + y, head)

    def signal(device):
        pl.semaphore_signal(barrier, inc=1, device_id=device, device_id_type=MESH)

    barrier = pltpu.get_barrier_semaphore()
    for d in range(1, ny):
        signal(on_y(lax.rem(y + d, ny)))
    for d in range(1, nz):
        signal(on_z(lax.rem(z + d, nz)))
    for d in range(1, nx):
        signal((seq, lax.rem(x + d, nx) * 2 + core))
    signal(sibling)
    for i in range(ny):

        @pl.when(off_diagonal | (i != y))
        def _():
            signal((head * ny + i, z))

    for i in range(nh):

        @pl.when(off_diagonal | (i != head))
        def _():
            signal((head * ny + y, i))

    loads = [
        pltpu.make_async_copy(src, dst, load_sem.at[n])
        for n, (src, dst) in enumerate(
            ((k_hbm, k_ref), (b_hbm, b_ref), (v_hbm, v_ref), (w_hbm, w_ref), (q_hbm, q_ref))
        )
    ]
    for load in loads:
        load.start()
    others = (ny - 1) + (nz - 1) + (nx - 1) + 1 + ny + nz
    pl.semaphore_wait(barrier, jnp.where(off_diagonal, others, others - 2))

    def half_a(i, arriving):
        return pltpu.make_async_remote_copy(
            src_ref=w_ref.at[:, pl.ds(0, dk)],
            dst_ref=wa.at[z, i] if arriving else wa.at[head, y],
            send_sem=a_send.at[i],
            recv_sem=a_recv.at[i if arriving else y],
            device_id=(head * ny + i, z),
            device_id_type=MESH,
        )

    def half_b(i, arriving):
        return pltpu.make_async_remote_copy(
            src_ref=w_ref.at[:, pl.ds(dk, dk)],
            dst_ref=wb.at[y, i if arriving else head],
            send_sem=b_send.at[i],
            recv_sem=b_recv.at[i if arriving else head],
            device_id=(i * ny + y, z),
            device_id_type=MESH,
        )

    def spread(action):
        for i in range(ny):

            @pl.when(off_diagonal | (i != y))
            def _():
                action(half_a, i)

        for i in range(nz):

            @pl.when(off_diagonal | (i != z))
            def _():
                action(half_b, i)

    loads[3].wait()
    spread(lambda half, i: half(i, 0).start())

    @pl.when(jnp.logical_not(off_diagonal))
    def _():
        wa[z, y] = w_ref[:, :dk]
        wb[y, z] = w_ref[:, dk:]

    wa_ring = Ring(nz, z, on_z, lambda i, p: wa.at[i, pl.ds(p * (ny // 2), ny // 2)], wa_send, wa_recv)
    wb_ring = Ring(ny, y, on_y, lambda i, p: wb.at[i, pl.ds(p * (nz // 2), nz // 2)], wb_send, wb_recv)

    def to_y(i, out, into, send, recv, arriving):
        return pltpu.make_async_remote_copy(
            src_ref=out.at[i],
            dst_ref=into.at[i if arriving else y],
            send_sem=send.at[i],
            recv_sem=recv.at[i if arriving else y],
            device_id=on_y(i),
            device_id_type=MESH,
        )

    def around_y(action):
        for i in range(ny):

            @pl.when(i != y)
            def _():
                action(i)

    def to_z(i, arriving):
        return pltpu.make_async_remote_copy(
            src_ref=m_out,
            dst_ref=m_in.at[i if arriving else z],
            send_sem=m_send.at[i],
            recv_sem=m_recv.at[i if arriving else z],
            device_id=on_z(i),
            device_id_type=MESH,
        )

    loads[0].wait()
    loads[1].wait()
    tok_id = lax.broadcasted_iota(jnp.int32, (refl, toks), 1)
    row_of = lax.broadcasted_iota(jnp.int32, (refl, toks), 0)
    ri = lax.broadcasted_iota(jnp.int32, (refl, refl), 0)
    ci = lax.broadcasted_iota(jnp.int32, (refl, refl), 1)
    keys, systems, gains, scales = [], [], [], []
    for h in range(heads):
        for j in (0, 1):
            k_int[h, pl.ds(j, toks, stride=2), :] = k_ref[j, :, h * dk : (h + 1) * dk].astype(F32)
    for h in range(heads):
        key = k_int[h]
        inv = lax.rsqrt(jnp.sum(key * key, axis=1, keepdims=True) + 1e-06)
        picked = jnp.where(
            lax.rem(row_of, 2) == 0, b_ref[0, h : h + 1, :], b_ref[1, h : h + 1, :]
        )
        beta = jnp.sum(jnp.where(row_of // 2 == tok_id, picked, 0.0), axis=1, keepdims=True)
        scales.append(beta * inv)
        gains.append(beta * inv * inv)
        kb = key.astype(BF16)
        keys.append(kb)
        systems.append(jnp.where(ri > ci, gains[h] * dot_nt(kb, kb), 0.0))
    eye = (ri == ci).astype(F32)
    inverses = [eye - jnp.where((ri >> 1) == (ci >> 1), a, 0.0) for a in systems]
    level = 1
    while (1 << level) < refl:
        here = ((ri >> (level + 1)) == (ci >> (level + 1))) & ((ri >> level) != (ci >> level))
        for h in range(heads):
            xb = inverses[h].astype(BF16)
            inner = dot(jnp.where(here, systems[h], 0.0).astype(BF16), xb)
            inverses[h] = inverses[h] - dot(xb, inner.astype(BF16))
        level += 1
    loads[2].wait()
    for h in range(heads):
        for j in (0, 1):
            v_int[h, pl.ds(j, toks, stride=2), :] = v_ref[j, :, h * dk : (h + 1) * dk].astype(F32)
    solved = []
    for h in range(heads):
        xs = split(inverses[h])
        residual = (eye - inverses[h]) - dot3(split(systems[h]), xs)
        fine = split(inverses[h] + dot(xs[0], residual.astype(BF16)))
        sides = jnp.concatenate([gains[h] * k_int[h], scales[h] * v_int[h]], axis=1)
        solved.append(dot3(fine, split(sides)))
    for h in range(heads):
        sh, slo = split(solved[h])
        moved = (dot_tn(sh, keys[h]) + dot_tn(slo, keys[h])).astype(BF16)
        for i in range(h, ny, heads):
            part = i // heads
            pay_out[i, :dk] = moved[:dk]
            pay_out[i, dk:] = moved[dk + part * sl : dk + (part + 1) * sl]
    around_y(lambda i: to_y(i, pay_out, pay_in, d_send, d_recv, 0).start())
    pay_in[y] = pay_out[y]
    for i in range(ny):

        @pl.when(off_diagonal | (i != y))
        def _():
            half_a(i, 1).wait_recv()

    wa_ring.hop(0)

    loads[4].wait()
    reach = (
        lax.broadcasted_iota(jnp.int32, (toks, refl), 1)
        <= 2 * lax.broadcasted_iota(jnp.int32, (toks, refl), 0) + 1
    )
    reads, locals_, q_inv = [], [], []
    for h in range(heads):
        qb = q_ref[:, h * dk : (h + 1) * dk]
        qf = qb.astype(F32)
        q_inv.append(lax.rsqrt(jnp.sum(qf * qf, axis=1, keepdims=True) + 1e-06))
        scores = jnp.where(reach, dot_nt(qb, keys[h]), 0.0)
        both = dot3(split(scores), split(solved[h]))
        reads.append((qf - both[:, :dk]).astype(BF16))
        locals_.append(both[:, dk:])

    top = (
        lax.broadcasted_iota(jnp.int32, (dk + sl, dk), 0)
        == lax.broadcasted_iota(jnp.int32, (dk + sl, dk), 1)
    ).astype(F32)
    bottom = lax.broadcasted_iota(jnp.int32, (dk + sl, dk), 0) >= dk
    stack = jnp.zeros((dk + sl, dk), F32)
    for i in range(ny):

        @pl.when(i != y)
        def _():
            to_y(i, pay_out, pay_in, d_send, d_recv, 1).wait_recv()

        e_all[:, i * dk : (i + 1) * dk] = stack[:dk].astype(BF16)
        s_pre[i] = stack[dk:]
        block = pay_in[i]
        grown = jnp.where(bottom, block.astype(F32), 0.0)
        stack = stack + dot((top - stack).astype(BF16), block[:dk]) + grown
    m_out[...] = stack.astype(BF16)
    for i in range(1, nz):

        @pl.when(i > z)
        def _():
            to_z(i, 0).start()

    wa_ring.hop(1)
    for i in range(nh):

        @pl.when(off_diagonal | (i != head))
        def _():
            half_b(i, 1).wait_recv()

    wb_ring.hop(0)
    state = jnp.zeros((sl, dk), F32)
    for i in range(nz - 1):

        @pl.when(i < z)
        def _():
            to_z(i, 1).wait_recv()

        block = m_in[i]
        after = state - dot(state.astype(BF16), block[:dk]) + block[dk:].astype(F32)
        state = jnp.where(i < z, after, state)
    drop = dot(state.astype(BF16), e_all[...])
    for i in range(ny):
        s_out[i] = (state - drop[:, i * dk : (i + 1) * dk] + s_pre[i]).astype(BF16)
    around_y(lambda i: to_y(i, s_out, s_in, s_send, s_recv, 0).start())
    s_in[y] = s_out[y]
    wa_ring.hop(2)
    wb_ring.hop(1)
    around_y(lambda i: to_y(i, s_out, s_in, s_send, s_recv, 1).wait_recv())

    def to_x(d, h, arriving):
        block = h_all.at[lax.rem(x + nx - d, nx) * 2 + core if arriving else head, h]
        return pltpu.make_async_remote_copy(
            src_ref=block,
            dst_ref=block,
            send_sem=x_send.at[d, h],
            recv_sem=x_recv.at[d, h],
            device_id=(seq, lax.rem(x + d, nx) * 2 + core),
            device_id_type=MESH,
        )

    def across(d, h, arriving):
        block = h_all.at[lax.rem(x + nx - d, nx) * 2 + (1 - core if arriving else core), h]
        return pltpu.make_async_remote_copy(
            src_ref=block,
            dst_ref=block,
            send_sem=c_send.at[d, h],
            recv_sem=c_recv.at[d, h],
            device_id=sibling,
            device_id_type=MESH,
        )

    distances = sorted(range(1, nx), key=lambda d: min(d, nx - d))
    for h in range(heads):
        carried = jnp.concatenate([s_in[i] for i in range(h, ny, heads)], axis=0)
        h_all[head, h] = (q_inv[h] * (dot_nt(reads[h], carried) + locals_[h])).astype(BF16)
        for d in distances:
            to_x(d, h, 0).start()
        across(0, h, 0).start()
    wa_ring.hop(3)
    wb_ring.hop(2)
    for d in distances:
        for h in range(heads):
            to_x(d, h, 1).wait_recv()
            across(d, h, 0).start()
    wb_ring.hop(3)
    wa_ring.hop(4)
    for d in [0] + distances:
        for h in range(heads):
            across(d, h, 1).wait_recv()
    wb_ring.hop(4)
    total = None
    for i in range(nh):
        left = jnp.concatenate([h_all[i, h] for h in range(heads)], axis=1)
        right = jnp.concatenate([wa[i].reshape(-1, dk), wb[:, i].reshape(-1, dk)], axis=1)
        term = dot_nt(left, right)
        total = term if total is None else total + term
    o_ref[...] = total.astype(BF16)

    spread(lambda half, i: half(i, 0).wait_send())
    wa_ring.finish()
    wb_ring.finish()
    around_y(lambda i: to_y(i, pay_out, pay_in, d_send, d_recv, 0).wait_send())
    around_y(lambda i: to_y(i, s_out, s_in, s_send, s_recv, 0).wait_send())
    for i in range(1, nz):

        @pl.when(i > z)
        def _():
            to_z(i, 0).wait_send()

    for h in range(heads):
        for d in distances:
            to_x(d, h, 0).wait_send()
        for d in [0] + distances:
            across(d, h, 0).wait_send()


def solution(mesh):
    nh = mesh.shape["head"]
    nz = nh
    ny = mesh.shape["seq"] // nz
    nx = nh // 2

    def per_device(queries, key_vectors, values, strengths, out_weight):
        toks = queries.shape[0]
        heads = strengths.shape[1]
        dk = queries.shape[1] // heads
        cols = out_weight.shape[1]
        sl = dk // (ny // heads)
        vmem, dma = pltpu.VMEM, pltpu.SemaphoreType.DMA

        def ring(n):
            return [dma((2, n // 2, 2))] * 2

        return pl.pallas_call(
            functools.partial(kernel, nz, ny, nh),
            out_shape=jax.ShapeDtypeStruct((toks, ny * cols), BF16),
            in_specs=[pl.BlockSpec(memory_space=pl.ANY)] * 5,
            out_specs=pl.BlockSpec(memory_space=pltpu.VMEM),
            scratch_shapes=[
                vmem(queries.shape, BF16),
                vmem(key_vectors.shape, BF16),
                vmem(values.shape, BF16),
                vmem(strengths.shape, F32),
                vmem((cols, heads * dk), BF16),
                vmem((heads, 2 * toks, dk), F32),
                vmem((heads, 2 * toks, dk), F32),
                vmem((nz, ny, cols, dk), BF16),
                vmem((ny, nz, cols, dk), BF16),
                vmem((ny, dk + sl, dk), BF16),
                vmem((ny, dk + sl, dk), BF16),
                vmem((dk + sl, dk), BF16),
                vmem((nz, dk + sl, dk), BF16),
                vmem((dk, ny * dk), BF16),
                vmem((ny, sl, dk), F32),
                vmem((ny, sl, dk), BF16),
                vmem((ny, sl, dk), BF16),
                vmem((nh, heads, toks, dk), BF16),
                dma((5,)),
                dma((ny,)),
                dma((ny,)),
                dma((nz,)),
                dma((nh,)),
                *ring(nz),
                *ring(ny),
                dma((ny,)),
                dma((ny,)),
                dma((nz,)),
                dma((nz,)),
                dma((ny,)),
                dma((ny,)),
                dma((nx, heads)),
                dma((nx, heads)),
                dma((nx, heads)),
                dma((nx, heads)),
            ],
            compiler_params=pltpu.CompilerParams(
                collective_id=0, has_side_effects=True, vmem_limit_bytes=62 * 1024 * 1024
            ),
        )(queries, key_vectors, values, strengths, out_weight.T)

    return jax.shard_map(
        per_device,
        mesh=mesh,
        in_specs=(
            P("seq", "head"),
            P(None, "seq", "head"),
            P(None, "seq", "head"),
            P(None, "head", "seq"),
            P("head", "seq"),
        ),
        out_specs=P("seq", "head"),
        check_vma=False,
    )
```

```python
import functools

import jax
import jax.numpy as jnp
from jax import lax
from jax.experimental import pallas as pl
from jax.experimental.pallas import tpu as pltpu
from jax.sharding import PartitionSpec as P

MESH = pl.DeviceIdType.MESH
F32 = jnp.float32
BF16 = jnp.bfloat16


def dot(a, b):
    return jnp.dot(a, b, preferred_element_type=F32)


def dot_nt(a, b):
    return lax.dot_general(a, b, (((1,), (1,)), ((), ())), preferred_element_type=F32)


def dot_tn(a, b):
    return lax.dot_general(a, b, (((0,), (0,)), ((), ())), preferred_element_type=F32)


def split(a):
    high = a.astype(BF16)
    return high, (a - high.astype(F32)).astype(BF16)


def dot3(a, b):
    return dot(a[0], b[0]) + (dot(a[1], b[0]) + dot(a[0], b[1]))


def far_first(n):
    return sorted(range(1, n), key=lambda d: -min(d, n - d))


class Ring:
    def __init__(self, n, place, device_at, slot, send, recv):
        self.n, self.place, self.device_at, self.slot = n, place, device_at, slot
        self.send, self.recv = send, recv

    def parts(self, hop, way):
        return (way,) if hop == self.n // 2 - 1 else (0, 1)

    def copy(self, hop, way, part, arriving):
        n, sign = self.n, (1, -1)[way]
        owner = lax.rem(self.place + 2 * n - sign * (hop + arriving), n)
        block = self.slot(owner, part)
        return pltpu.make_async_remote_copy(
            src_ref=block,
            dst_ref=block,
            send_sem=self.send.at[way, hop, part],
            recv_sem=self.recv.at[way, hop, part],
            device_id=self.device_at(lax.rem(self.place + n + sign, n)),
            device_id_type=MESH,
        )

    def hop(self, hop):
        if hop > self.n // 2:
            return
        for part in (0, 1):
            for way in (0, 1):
                if hop > 0 and part in self.parts(hop - 1, way):
                    self.copy(hop - 1, way, part, 1).wait_recv()
                if hop < self.n // 2 and part in self.parts(hop, way):
                    self.copy(hop, way, part, 0).start()

    def finish(self):
        for hop in range(self.n // 2):
            for way in (0, 1):
                for part in self.parts(hop, way):
                    self.copy(hop, way, part, 0).wait_send()


def kernel(
    nz, ny, nh,
    q_hbm, k_hbm, v_hbm, b_hbm, w_hbm, o_ref,
    q_ref, k_ref, v_ref, b_ref, w_ref, k_int, v_int, wa, wb, pay_out, pay_in, m_out, m_in, e_all, s_pre, s_out, s_in, h_all,
    load_sem, a_send, a_recv, b_send, b_recv, wa_send, wa_recv, wb_send, wb_recv,
    d_send, d_recv, m_send, m_recv, s_send, s_recv, x_send, x_recv, c_send, c_recv,
):
    seq, head = lax.axis_index("seq"), lax.axis_index("head")
    z, y = seq // ny, lax.rem(seq, ny)
    x, core = head // 2, lax.rem(head, 2)
    nx = nh // 2
    heads = b_ref.shape[1]
    toks = q_ref.shape[0]
    dk = q_ref.shape[1] // heads
    refl = 2 * toks
    per = ny // heads
    sl = dk // per
    off_diagonal = z != head
    sibling = (seq, x * 2 + 1 - core)

    def on_y(i):
        return (z * ny + i, head)

    def on_z(i):
        return (i * ny + y, head)

    def signal(device):
        pl.semaphore_signal(barrier, inc=1, device_id=device, device_id_type=MESH)

    barrier = pltpu.get_barrier_semaphore()
    for d in range(1, ny):
        signal(on_y(lax.rem(y + d, ny)))
    for d in range(1, nz):
        signal(on_z(lax.rem(z + d, nz)))
    for d in range(1, nx):
        signal((seq, lax.rem(x + d, nx) * 2 + core))
    signal(sibling)
    for d in range(1, ny):
        signal((head * ny + lax.rem(y + d, ny), z))
    for d in range(1, nh):
        signal((head * ny + y, lax.rem(z + d, nh)))

    @pl.when(off_diagonal)
    def _():
        signal((head * ny + y, z))
        signal((head * ny + y, z))

    loads = [
        pltpu.make_async_copy(src, dst, load_sem.at[n])
        for n, (src, dst) in enumerate(
            ((k_hbm, k_ref), (b_hbm, b_ref), (v_hbm, v_ref), (w_hbm, w_ref), (q_hbm, q_ref))
        )
    ]
    for load in loads:
        load.start()
    others = (ny - 1) + (nz - 1) + (nx - 1) + 1 + ny + nz
    pl.semaphore_wait(barrier, jnp.where(off_diagonal, others, others - 2))

    def half_a(d, arriving):
        other = lax.rem(y + ny - d, ny)
        return pltpu.make_async_remote_copy(
            src_ref=w_ref.at[:, pl.ds(0, dk)],
            dst_ref=wa.at[z, other] if arriving else wa.at[head, y],
            send_sem=a_send.at[d],
            recv_sem=a_recv.at[d],
            device_id=(head * ny + lax.rem(y + d, ny), z),
            device_id_type=MESH,
        )

    def half_b(d, arriving):
        other = lax.rem(z + nz - d, nz)
        return pltpu.make_async_remote_copy(
            src_ref=w_ref.at[:, pl.ds(dk, dk)],
            dst_ref=wb.at[y, other if arriving else head],
            send_sem=b_send.at[d],
            recv_sem=b_recv.at[d],
            device_id=(lax.rem(head + d, nz) * ny + y, z),
            device_id_type=MESH,
        )

    def spread(action, copies):
        for half, n in copies:
            for d in far_first(n):
                action(half, d)

        @pl.when(off_diagonal)
        def _():
            for half, _ in copies:
                action(half, 0)

    both_halves = ((half_a, ny), (half_b, nz))
    loads[3].wait()
    spread(lambda half, d: half(d, 0).start(), both_halves)

    @pl.when(jnp.logical_not(off_diagonal))
    def _():
        wa[z, y] = w_ref[:, :dk]
        wb[y, z] = w_ref[:, dk:]

    wa_ring = Ring(nz, z, on_z, lambda i, p: wa.at[i, pl.ds(p * (ny // 2), ny // 2)], wa_send, wa_recv)
    wb_ring = Ring(ny, y, on_y, lambda i, p: wb.at[i, pl.ds(p * (nz // 2), nz // 2)], wb_send, wb_recv)

    def to_y(d, out, into, send, recv, arriving):
        peer, other = lax.rem(y + d, ny), lax.rem(y + ny - d, ny)
        return pltpu.make_async_remote_copy(
            src_ref=out.at[peer],
            dst_ref=into.at[other if arriving else y],
            send_sem=send.at[d],
            recv_sem=recv.at[d],
            device_id=on_y(peer),
            device_id_type=MESH,
        )

    def around_y(action):
        for d in far_first(ny):
            action(d)

    def to_z(i, arriving):
        return pltpu.make_async_remote_copy(
            src_ref=m_out,
            dst_ref=m_in.at[i if arriving else z],
            send_sem=m_send.at[i],
            recv_sem=m_recv.at[i if arriving else z],
            device_id=on_z(i),
            device_id_type=MESH,
        )

    loads[0].wait()
    loads[1].wait()
    tok_id = lax.broadcasted_iota(jnp.int32, (refl, toks), 1)
    row_of = lax.broadcasted_iota(jnp.int32, (refl, toks), 0)
    ri = lax.broadcasted_iota(jnp.int32, (refl, refl), 0)
    ci = lax.broadcasted_iota(jnp.int32, (refl, refl), 1)
    keys, systems, gains, scales = [], [], [], []
    for h in range(heads):
        for j in (0, 1):
            k_int[h, pl.ds(j, toks, stride=2), :] = k_ref[j, :, h * dk : (h + 1) * dk].astype(F32)
    for h in range(heads):
        key = k_int[h]
        inv = lax.rsqrt(jnp.sum(key * key, axis=1, keepdims=True) + 1e-06)
        picked = jnp.where(
            lax.rem(row_of, 2) == 0, b_ref[0, h : h + 1, :], b_ref[1, h : h + 1, :]
        )
        beta = jnp.sum(jnp.where(row_of // 2 == tok_id, picked, 0.0), axis=1, keepdims=True)
        scales.append(beta * inv)
        gains.append(beta * inv * inv)
        kb = key.astype(BF16)
        keys.append(kb)
        systems.append(jnp.where(ri > ci, gains[h] * dot_nt(kb, kb), 0.0))
    eye = (ri == ci).astype(F32)
    half = refl // 2
    ri2, ci2, eye2 = ri[:half, :half], ci[:half, :half], eye[:half, :half]
    blocks = [a[o : o + half, o : o + half] for a in systems for o in (0, half)]
    parts = [eye2 - jnp.where((ri2 >> 1) == (ci2 >> 1), a, 0.0) for a in blocks]
    level = 1
    while (1 << level) < half:
        here = ((ri2 >> (level + 1)) == (ci2 >> (level + 1))) & ((ri2 >> level) != (ci2 >> level))
        narrow = [p.astype(BF16) for p in parts]
        inner = [
            dot(jnp.where(here, a, 0.0).astype(BF16), p) for a, p in zip(blocks, narrow)
        ]
        parts = [p - dot(b, i.astype(BF16)) for p, b, i in zip(parts, narrow, inner)]
        level += 1
    inverses = []
    for h in range(heads):
        first, second = parts[2 * h], parts[2 * h + 1]
        inner = dot(systems[h][half:, :half].astype(BF16), first.astype(BF16))
        corner = -dot(second.astype(BF16), inner.astype(BF16))
        inverses.append(
            jnp.concatenate(
                [
                    jnp.concatenate([first, jnp.zeros_like(first)], axis=1),
                    jnp.concatenate([corner, second], axis=1),
                ],
                axis=0,
            )
        )
    loads[2].wait()
    for h in range(heads):
        for j in (0, 1):
            v_int[h, pl.ds(j, toks, stride=2), :] = v_ref[j, :, h * dk : (h + 1) * dk].astype(F32)
    solved = []
    for h in range(heads):
        xs = split(inverses[h])
        residual = (eye - inverses[h]) - dot3(split(systems[h]), xs)
        fine = split(inverses[h] + dot(xs[0], residual.astype(BF16)))
        sides = jnp.concatenate([gains[h] * k_int[h], scales[h] * v_int[h]], axis=1)
        solved.append(dot3(fine, split(sides)))
    for h in range(heads):
        sh, slo = split(solved[h])
        moved = (dot_tn(sh, keys[h]) + dot_tn(slo, keys[h])).astype(BF16)
        for i in range(h, ny, heads):
            part = i // heads
            pay_out[i, :dk] = moved[:dk]
            pay_out[i, dk:] = moved[dk + part * sl : dk + (part + 1) * sl]
    around_y(lambda d: to_y(d, pay_out, pay_in, d_send, d_recv, 0).start())
    pay_in[y] = pay_out[y]
    loads[4].wait()
    reach = (
        lax.broadcasted_iota(jnp.int32, (toks, refl), 1)
        <= 2 * lax.broadcasted_iota(jnp.int32, (toks, refl), 0) + 1
    )
    reads, locals_, q_inv = [], [], []
    for h in range(heads):
        qb = q_ref[:, h * dk : (h + 1) * dk]
        qf = qb.astype(F32)
        q_inv.append(lax.rsqrt(jnp.sum(qf * qf, axis=1, keepdims=True) + 1e-06))
        scores = jnp.where(reach, dot_nt(qb, keys[h]), 0.0)
        both = dot3(split(scores), split(solved[h]))
        reads.append((qf - both[:, :dk]).astype(BF16))
        locals_.append(both[:, dk:])

    spread(lambda half, d: half(d, 1).wait_recv(), both_halves[:1])
    wa_ring.hop(0)
    top = (
        lax.broadcasted_iota(jnp.int32, (dk + sl, dk), 0)
        == lax.broadcasted_iota(jnp.int32, (dk + sl, dk), 1)
    ).astype(F32)
    bottom = lax.broadcasted_iota(jnp.int32, (dk + sl, dk), 0) >= dk

    def join(earlier, later):
        moved = dot((top - earlier).astype(BF16), later[:dk].astype(BF16))
        return earlier + moved + jnp.where(bottom, later, 0.0)

    def prefixes(terms):
        done = [terms[0]]
        for term in terms[1:]:
            done.append(join(done[-1], term))
        return done

    around = far_first(ny)[::-1]
    for n, d in enumerate(around):
        to_y(d, pay_out, pay_in, d_send, d_recv, 1).wait_recv()
    spread(lambda half, d: half(d, 1).wait_recv(), both_halves[1:])
    wb_ring.hop(0)
    upto = prefixes([pay_in[i].astype(F32) for i in range(ny)])
    m_out[...] = upto[-1].astype(BF16)
    for d in range(nz - 1, 0, -1):

        @pl.when(z + d < nz)
        def _():
            to_z(z + d, 0).start()

    wa_ring.hop(1)

    for i in range(ny):
        stack = upto[i - 1] if i > 0 else jnp.zeros((dk + sl, dk), F32)
        e_all[:, i * dk : (i + 1) * dk] = stack[:dk].astype(BF16)
        s_pre[i] = stack[dk:]
    wb_ring.hop(1)
    for i in range(nz - 1):

        @pl.when(i < z)
        def _():
            to_z(i, 1).wait_recv()

    rows_in = [jnp.where(i < z, m_in[i].astype(F32), 0.0) for i in range(nz - 1)]

    def middle_of(terms):
        return 1 << ((len(terms) - 1).bit_length() - 1)

    def whole(terms):
        if len(terms) == 1:
            return terms[0]
        middle = middle_of(terms)
        return join(whole(terms[:middle]), whole(terms[middle:]))

    def state_after(terms):
        if len(terms) == 1:
            return terms[0][dk:]
        middle = middle_of(terms)
        earlier, later = state_after(terms[:middle]), whole(terms[middle:])
        return earlier - dot(earlier.astype(BF16), later[:dk].astype(BF16)) + later[dk:]

    state = state_after(rows_in)
    drop = dot(state.astype(BF16), e_all[...])
    for i in range(ny):
        s_out[i] = (state - drop[:, i * dk : (i + 1) * dk] + s_pre[i]).astype(BF16)
    around_y(lambda d: to_y(d, s_out, s_in, s_send, s_recv, 0).start())
    s_in[y] = s_out[y]
    wa_ring.hop(2)
    wb_ring.hop(2)
    around_y(lambda d: to_y(d, s_out, s_in, s_send, s_recv, 1).wait_recv())

    def to_x(d, h, arriving):
        block = h_all.at[lax.rem(x + nx - d, nx) * 2 + core if arriving else head, h]
        return pltpu.make_async_remote_copy(
            src_ref=block,
            dst_ref=block,
            send_sem=x_send.at[d, h],
            recv_sem=x_recv.at[d, h],
            device_id=(seq, lax.rem(x + d, nx) * 2 + core),
            device_id_type=MESH,
        )

    def across(d, h, arriving):
        block = h_all.at[lax.rem(x + nx - d, nx) * 2 + (1 - core if arriving else core), h]
        return pltpu.make_async_remote_copy(
            src_ref=block,
            dst_ref=block,
            send_sem=c_send.at[d, h],
            recv_sem=c_recv.at[d, h],
            device_id=sibling,
            device_id_type=MESH,
        )

    distances = far_first(nx)
    for h in range(heads):
        carried = jnp.concatenate([s_in[i] for i in range(h, ny, heads)], axis=0)
        h_all[head, h] = (q_inv[h] * (dot_nt(reads[h], carried) + locals_[h])).astype(BF16)
        for d in distances:
            to_x(d, h, 0).start()
        across(0, h, 0).start()
    distances = distances[::-1]
    wa_ring.hop(3)
    wb_ring.hop(3)
    for d in distances:
        for h in range(heads):
            to_x(d, h, 1).wait_recv()
            across(d, h, 0).start()
    wa_ring.hop(4)
    wb_ring.hop(4)

    def term(d, which):
        i = lax.rem(x + nx - d, nx) * 2 + which
        left = jnp.concatenate([h_all[i, h] for h in range(heads)], axis=1)
        right = jnp.concatenate([wa[i].reshape(-1, dk), wb[:, i].reshape(-1, dk)], axis=1)
        return dot_nt(left, right)

    total = term(0, core)
    for d in distances:
        total = total + term(d, core)
    for d in [0] + distances:
        for h in range(heads):
            across(d, h, 1).wait_recv()
        total = total + term(d, 1 - core)
    o_ref[...] = total.astype(BF16)

    spread(lambda half, d: half(d, 0).wait_send(), both_halves)
    wa_ring.finish()
    wb_ring.finish()
    around_y(lambda d: to_y(d, pay_out, pay_in, d_send, d_recv, 0).wait_send())
    around_y(lambda d: to_y(d, s_out, s_in, s_send, s_recv, 0).wait_send())
    for i in range(1, nz):

        @pl.when(i > z)
        def _():
            to_z(i, 0).wait_send()

    for h in range(heads):
        for d in distances:
            to_x(d, h, 0).wait_send()
        for d in [0] + distances:
            across(d, h, 0).wait_send()


def solution(mesh):
    nh = mesh.shape["head"]
    nz = nh
    ny = mesh.shape["seq"] // nz
    nx = nh // 2

    def per_device(queries, key_vectors, values, strengths, out_weight):
        toks = queries.shape[0]
        heads = strengths.shape[1]
        dk = queries.shape[1] // heads
        cols = out_weight.shape[1]
        sl = dk // (ny // heads)
        vmem, dma = pltpu.VMEM, pltpu.SemaphoreType.DMA

        def ring(n):
            return [dma((2, n // 2, 2))] * 2

        return pl.pallas_call(
            functools.partial(kernel, nz, ny, nh),
            out_shape=jax.ShapeDtypeStruct((toks, ny * cols), BF16),
            in_specs=[pl.BlockSpec(memory_space=pl.ANY)] * 5,
            out_specs=pl.BlockSpec(memory_space=pltpu.VMEM),
            scratch_shapes=[
                vmem(queries.shape, BF16),
                vmem(key_vectors.shape, BF16),
                vmem(values.shape, BF16),
                vmem(strengths.shape, F32),
                vmem((cols, heads * dk), BF16),
                vmem((heads, 2 * toks, dk), F32),
                vmem((heads, 2 * toks, dk), F32),
                vmem((nz, ny, cols, dk), BF16),
                vmem((ny, nz, cols, dk), BF16),
                vmem((ny, dk + sl, dk), BF16),
                vmem((ny, dk + sl, dk), BF16),
                vmem((dk + sl, dk), BF16),
                vmem((nz, dk + sl, dk), BF16),
                vmem((dk, ny * dk), BF16),
                vmem((ny, sl, dk), F32),
                vmem((ny, sl, dk), BF16),
                vmem((ny, sl, dk), BF16),
                vmem((nh, heads, toks, dk), BF16),
                dma((5,)),
                dma((ny,)),
                dma((ny,)),
                dma((nz,)),
                dma((nh,)),
                *ring(nz),
                *ring(ny),
                dma((ny,)),
                dma((ny,)),
                dma((nz,)),
                dma((nz,)),
                dma((ny,)),
                dma((ny,)),
                dma((nx, heads)),
                dma((nx, heads)),
                dma((nx, heads)),
                dma((nx, heads)),
            ],
            compiler_params=pltpu.CompilerParams(
                collective_id=0, has_side_effects=True, vmem_limit_bytes=62 * 1024 * 1024
            ),
        )(queries, key_vectors, values, strengths, out_weight.T)

    return jax.shard_map(
        per_device,
        mesh=mesh,
        in_specs=(
            P("seq", "head"),
            P(None, "seq", "head"),
            P(None, "seq", "head"),
            P(None, "head", "seq"),
            P("head", "seq"),
        ),
        out_specs=P("seq", "head"),
        check_vma=False,
    )
```

```python
import functools

import jax
import jax.numpy as jnp
from jax import lax
from jax.experimental import pallas as pl
from jax.experimental.pallas import tpu as pltpu
from jax.sharding import PartitionSpec as P

MESH = pl.DeviceIdType.MESH
F32 = jnp.float32
BF16 = jnp.bfloat16


def dot(a, b):
    return jnp.dot(a, b, preferred_element_type=F32)


def dot_nt(a, b):
    return lax.dot_general(a, b, (((1,), (1,)), ((), ())), preferred_element_type=F32)


def dot_tn(a, b):
    return lax.dot_general(a, b, (((0,), (0,)), ((), ())), preferred_element_type=F32)


def split(a):
    high = a.astype(BF16)
    return high, (a - high.astype(F32)).astype(BF16)


def dot3(a, b):
    return dot(a[0], b[0]) + (dot(a[1], b[0]) + dot(a[0], b[1]))


def far_first(n):
    return sorted(range(1, n), key=lambda d: -min(d, n - d))


class Ring:
    def __init__(self, n, place, device_at, slot, send, recv):
        self.n, self.place, self.device_at, self.slot = n, place, device_at, slot
        self.send, self.recv = send, recv

    def parts(self, hop, way):
        return (way,) if hop == self.n // 2 - 1 else (0, 1)

    def copy(self, hop, way, part, arriving):
        n, sign = self.n, (1, -1)[way]
        owner = lax.rem(self.place + 2 * n - sign * (hop + arriving), n)
        block = self.slot(owner, part)
        return pltpu.make_async_remote_copy(
            src_ref=block,
            dst_ref=block,
            send_sem=self.send.at[way, hop, part],
            recv_sem=self.recv.at[way, hop, part],
            device_id=self.device_at(lax.rem(self.place + n + sign, n)),
            device_id_type=MESH,
        )

    def hop(self, hop):
        if hop > self.n // 2:
            return
        for part in (0, 1):
            for way in (0, 1):
                if hop > 0 and part in self.parts(hop - 1, way):
                    self.copy(hop - 1, way, part, 1).wait_recv()
                if hop < self.n // 2 and part in self.parts(hop, way):
                    self.copy(hop, way, part, 0).start()

    def finish(self):
        for hop in range(self.n // 2):
            for way in (0, 1):
                for part in self.parts(hop, way):
                    self.copy(hop, way, part, 0).wait_send()


def kernel(
    nz, ny, nh,
    q_hbm, k_hbm, v_hbm, b_hbm, w_hbm, o_ref,
    q_ref, k_ref, v_ref, b_ref, w_ref, k_int, v_int, wa, wb, pay_out, pay_in, m_out, m_in, e_all, s_pre, s_out, s_in, h_all,
    load_sem, a_send, a_recv, b_send, b_recv, wa_send, wa_recv, wb_send, wb_recv,
    d_send, d_recv, m_send, m_recv, s_send, s_recv, x_send, x_recv, c_send, c_recv,
):
    seq, head = lax.axis_index("seq"), lax.axis_index("head")
    z, y = seq // ny, lax.rem(seq, ny)
    x, core = head // 2, lax.rem(head, 2)
    nx = nh // 2
    heads = b_ref.shape[1]
    toks = q_ref.shape[0]
    dk = q_ref.shape[1] // heads
    refl = 2 * toks
    per = ny // heads
    sl = dk // per
    off_diagonal = z != head
    sibling = (seq, x * 2 + 1 - core)

    def on_y(i):
        return (z * ny + i, head)

    def on_z(i):
        return (i * ny + y, head)

    def signal(device):
        pl.semaphore_signal(barrier, inc=1, device_id=device, device_id_type=MESH)

    loads = [
        pltpu.make_async_copy(src, dst, load_sem.at[n])
        for n, (src, dst) in enumerate(
            ((k_hbm, k_ref), (b_hbm, b_ref), (v_hbm, v_ref), (w_hbm, w_ref), (q_hbm, q_ref))
        )
    ]
    for load in loads:
        load.start()

    barrier = pltpu.get_barrier_semaphore()
    for d in range(1, ny):
        signal(on_y(lax.rem(y + d, ny)))
    for d in range(1, nz):
        signal(on_z(lax.rem(z + d, nz)))
    for d in range(1, nx):
        signal((seq, lax.rem(x + d, nx) * 2 + core))
    signal(sibling)
    for d in range(1, nh):
        signal((head * ny + y, lax.rem(z + d, nh)))

    @pl.when(off_diagonal)
    def _():
        signal((head * ny + y, z))
        signal((head * ny + y, z))

    def half_a(d, arriving):
        other = lax.rem(y + ny - d, ny)
        if d == 0:
            src, dst = w_ref.at[:, pl.ds(0, dk)], wa.at[z, y] if arriving else wa.at[head, y]
            device = (head * ny + y, z)
        else:
            src = dst = wa.at[z, other if arriving else y]
            device = on_y(lax.rem(y + d, ny))
        return pltpu.make_async_remote_copy(
            src_ref=src,
            dst_ref=dst,
            send_sem=a_send.at[d],
            recv_sem=a_recv.at[d],
            device_id=device,
            device_id_type=MESH,
        )

    def half_b(d, arriving):
        other = lax.rem(z + nz - d, nz)
        return pltpu.make_async_remote_copy(
            src_ref=w_ref.at[:, pl.ds(dk, dk)],
            dst_ref=wb.at[y, other if arriving else head],
            send_sem=b_send.at[d],
            recv_sem=b_recv.at[d],
            device_id=(lax.rem(head + d, nz) * ny + y, z),
            device_id_type=MESH,
        )

    def spread(action, copies):
        for half, n in copies:
            for d in far_first(n):
                action(half, d)

        @pl.when(off_diagonal)
        def _():
            for half, _ in copies:
                action(half, 0)

    both_halves = ((half_a, 1), (half_b, nz))
    wa_ring = Ring(nz, z, on_z, lambda i, p: wa.at[i, pl.ds(p * (ny // 2), ny // 2)], wa_send, wa_recv)
    wb_ring = Ring(ny, y, on_y, lambda i, p: wb.at[i, pl.ds(p * (nz // 2), nz // 2)], wb_send, wb_recv)

    def to_y(d, out, into, send, recv, arriving):
        peer, other = lax.rem(y + d, ny), lax.rem(y + ny - d, ny)
        return pltpu.make_async_remote_copy(
            src_ref=out.at[peer],
            dst_ref=into.at[other if arriving else y],
            send_sem=send.at[d],
            recv_sem=recv.at[d],
            device_id=on_y(peer),
            device_id_type=MESH,
        )

    def around_y(action):
        for d in far_first(ny):
            action(d)

    def to_z(i, arriving):
        return pltpu.make_async_remote_copy(
            src_ref=m_out,
            dst_ref=m_in.at[i if arriving else z],
            send_sem=m_send.at[i],
            recv_sem=m_recv.at[i if arriving else z],
            device_id=on_z(i),
            device_id_type=MESH,
        )

    loads[0].wait()
    loads[1].wait()
    tok_id = lax.broadcasted_iota(jnp.int32, (refl, toks), 1)
    row_of = lax.broadcasted_iota(jnp.int32, (refl, toks), 0)
    ri = lax.broadcasted_iota(jnp.int32, (refl, refl), 0)
    ci = lax.broadcasted_iota(jnp.int32, (refl, refl), 1)
    keys, systems, gains, scales = [], [], [], []
    for h in range(heads):
        for j in (0, 1):
            k_int[h, pl.ds(j, toks, stride=2), :] = k_ref[j, :, h * dk : (h + 1) * dk].astype(F32)
    for h in range(heads):
        key = k_int[h]
        inv = lax.rsqrt(jnp.sum(key * key, axis=1, keepdims=True) + 1e-06)
        picked = jnp.where(
            lax.rem(row_of, 2) == 0, b_ref[0, h : h + 1, :], b_ref[1, h : h + 1, :]
        )
        beta = jnp.sum(jnp.where(row_of // 2 == tok_id, picked, 0.0), axis=1, keepdims=True)
        scales.append(beta * inv)
        gains.append(beta * inv * inv)
        kb = key.astype(BF16)
        keys.append(kb)
        systems.append(jnp.where(ri > ci, gains[h] * dot_nt(kb, kb), 0.0))
    eye = (ri == ci).astype(F32)
    half = refl // 2
    ri2, ci2, eye2 = ri[:half, :half], ci[:half, :half], eye[:half, :half]
    blocks = [a[o : o + half, o : o + half] for a in systems for o in (0, half)]
    parts = [eye2 - jnp.where((ri2 >> 1) == (ci2 >> 1), a, 0.0) for a in blocks]
    level = 1
    while (1 << level) < half:
        here = ((ri2 >> (level + 1)) == (ci2 >> (level + 1))) & ((ri2 >> level) != (ci2 >> level))
        narrow = [p.astype(BF16) for p in parts]
        inner = [
            dot(jnp.where(here, a, 0.0).astype(BF16), p) for a, p in zip(blocks, narrow)
        ]
        parts = [p - dot(b, i.astype(BF16)) for p, b, i in zip(parts, narrow, inner)]
        level += 1
    others = (ny - 1) + (nz - 1) + (nx - 1) + 1 + 1 + nz
    pl.semaphore_wait(barrier, jnp.where(off_diagonal, others, others - 2))

    loads[3].wait()
    spread(lambda half, d: half(d, 0).start(), both_halves)

    @pl.when(jnp.logical_not(off_diagonal))
    def _():
        wa[z, y] = w_ref[:, :dk]
        wb[y, z] = w_ref[:, dk:]

    inverses = []
    for h in range(heads):
        first, second = parts[2 * h], parts[2 * h + 1]
        inner = dot(systems[h][half:, :half].astype(BF16), first.astype(BF16))
        corner = -dot(second.astype(BF16), inner.astype(BF16))
        inverses.append(
            jnp.concatenate(
                [
                    jnp.concatenate([first, jnp.zeros_like(first)], axis=1),
                    jnp.concatenate([corner, second], axis=1),
                ],
                axis=0,
            )
        )
    loads[2].wait()
    for h in range(heads):
        for j in (0, 1):
            v_int[h, pl.ds(j, toks, stride=2), :] = v_ref[j, :, h * dk : (h + 1) * dk].astype(F32)
    solved = []
    for h in range(heads):
        xs = split(inverses[h])
        residual = (eye - inverses[h]) - dot3(split(systems[h]), xs)
        fine = split(inverses[h] + dot(xs[0], residual.astype(BF16)))
        sides = jnp.concatenate([gains[h] * k_int[h], scales[h] * v_int[h]], axis=1)
        solved.append(dot3(fine, split(sides)))
    for h in range(heads):
        sh, slo = split(solved[h])
        moved = (dot_tn(sh, keys[h]) + dot_tn(slo, keys[h])).astype(BF16)
        for i in range(h, ny, heads):
            part = i // heads
            pay_out[i, :dk] = moved[:dk]
            pay_out[i, dk:] = moved[dk + part * sl : dk + (part + 1) * sl]
    around_y(lambda d: to_y(d, pay_out, pay_in, d_send, d_recv, 0).start())
    pay_in[y] = pay_out[y]
    spread(lambda half, d: half(d, 1).wait_recv(), both_halves[:1])
    for d in far_first(ny):
        half_a(d, 0).start()
    loads[4].wait()
    reach = (
        lax.broadcasted_iota(jnp.int32, (toks, refl), 1)
        <= 2 * lax.broadcasted_iota(jnp.int32, (toks, refl), 0) + 1
    )
    reads, locals_, q_inv = [], [], []
    for h in range(heads):
        qb = q_ref[:, h * dk : (h + 1) * dk]
        qf = qb.astype(F32)
        q_inv.append(lax.rsqrt(jnp.sum(qf * qf, axis=1, keepdims=True) + 1e-06))
        scores = jnp.where(reach, dot_nt(qb, keys[h]), 0.0)
        both = dot3(split(scores), split(solved[h]))
        reads.append((qf - both[:, :dk]).astype(BF16))
        locals_.append(both[:, dk:])

    for d in far_first(ny)[::-1]:
        half_a(d, 1).wait_recv()
    wa_ring.hop(0)
    top = (
        lax.broadcasted_iota(jnp.int32, (dk + sl, dk), 0)
        == lax.broadcasted_iota(jnp.int32, (dk + sl, dk), 1)
    ).astype(F32)
    bottom = lax.broadcasted_iota(jnp.int32, (dk + sl, dk), 0) >= dk

    def join(earlier, later):
        moved = dot((top - earlier).astype(BF16), later[:dk].astype(BF16))
        return earlier + moved + jnp.where(bottom, later, 0.0)

    def prefixes(terms):
        done = [terms[0]]
        for term in terms[1:]:
            done.append(join(done[-1], term))
        return done

    around = far_first(ny)[::-1]
    for n, d in enumerate(around):
        to_y(d, pay_out, pay_in, d_send, d_recv, 1).wait_recv()
    spread(lambda half, d: half(d, 1).wait_recv(), both_halves[1:])
    wb_ring.hop(0)
    upto = prefixes([pay_in[i].astype(F32) for i in range(ny)])
    m_out[...] = upto[-1].astype(BF16)
    for d in range(nz - 1, 0, -1):

        @pl.when(z + d < nz)
        def _():
            to_z(z + d, 0).start()

    wa_ring.hop(1)

    for i in range(ny):
        stack = upto[i - 1] if i > 0 else jnp.zeros((dk + sl, dk), F32)
        e_all[:, i * dk : (i + 1) * dk] = stack[:dk].astype(BF16)
        s_pre[i] = stack[dk:]
    wb_ring.hop(1)
    for i in range(nz - 1):

        @pl.when(i < z)
        def _():
            to_z(i, 1).wait_recv()

    rows_in = [jnp.where(i < z, m_in[i].astype(F32), 0.0) for i in range(nz - 1)]

    def middle_of(terms):
        return 1 << ((len(terms) - 1).bit_length() - 1)

    def whole(terms):
        if len(terms) == 1:
            return terms[0]
        middle = middle_of(terms)
        return join(whole(terms[:middle]), whole(terms[middle:]))

    def state_after(terms):
        if len(terms) == 1:
            return terms[0][dk:]
        middle = middle_of(terms)
        earlier, later = state_after(terms[:middle]), whole(terms[middle:])
        return earlier - dot(earlier.astype(BF16), later[:dk].astype(BF16)) + later[dk:]

    state = state_after(rows_in)
    drop = dot(state.astype(BF16), e_all[...])
    for i in range(ny):
        s_out[i] = (state - drop[:, i * dk : (i + 1) * dk] + s_pre[i]).astype(BF16)
    around_y(lambda d: to_y(d, s_out, s_in, s_send, s_recv, 0).start())
    s_in[y] = s_out[y]
    wa_ring.hop(2)
    wb_ring.hop(2)
    around_y(lambda d: to_y(d, s_out, s_in, s_send, s_recv, 1).wait_recv())

    def to_x(d, h, arriving):
        block = h_all.at[lax.rem(x + nx - d, nx) * 2 + core if arriving else head, h]
        return pltpu.make_async_remote_copy(
            src_ref=block,
            dst_ref=block,
            send_sem=x_send.at[d, h],
            recv_sem=x_recv.at[d, h],
            device_id=(seq, lax.rem(x + d, nx) * 2 + core),
            device_id_type=MESH,
        )

    def across(d, h, arriving):
        block = h_all.at[lax.rem(x + nx - d, nx) * 2 + (1 - core if arriving else core), h]
        return pltpu.make_async_remote_copy(
            src_ref=block,
            dst_ref=block,
            send_sem=c_send.at[d, h],
            recv_sem=c_recv.at[d, h],
            device_id=sibling,
            device_id_type=MESH,
        )

    distances = far_first(nx)
    for h in range(heads):
        carried = jnp.concatenate([s_in[i] for i in range(h, ny, heads)], axis=0)
        h_all[head, h] = (q_inv[h] * (dot_nt(reads[h], carried) + locals_[h])).astype(BF16)
        for d in distances:
            to_x(d, h, 0).start()
        across(0, h, 0).start()
    distances = distances[::-1]
    wa_ring.hop(3)
    wb_ring.hop(3)
    for d in distances:
        for h in range(heads):
            to_x(d, h, 1).wait_recv()
            across(d, h, 0).start()
    wa_ring.hop(4)
    wb_ring.hop(4)

    def term(d, which):
        i = lax.rem(x + nx - d, nx) * 2 + which
        left = jnp.concatenate([h_all[i, h] for h in range(heads)], axis=1)
        right = jnp.concatenate([wa[i].reshape(-1, dk), wb[:, i].reshape(-1, dk)], axis=1)
        return dot_nt(left, right)

    total = term(0, core)
    for d in distances:
        total = total + term(d, core)
    for d in [0] + distances:
        for h in range(heads):
            across(d, h, 1).wait_recv()
        total = total + term(d, 1 - core)
    o_ref[...] = total.astype(BF16)

    spread(lambda half, d: half(d, 0).wait_send(), both_halves)
    for d in far_first(ny):
        half_a(d, 0).wait_send()
    wa_ring.finish()
    wb_ring.finish()
    around_y(lambda d: to_y(d, pay_out, pay_in, d_send, d_recv, 0).wait_send())
    around_y(lambda d: to_y(d, s_out, s_in, s_send, s_recv, 0).wait_send())
    for i in range(1, nz):

        @pl.when(i > z)
        def _():
            to_z(i, 0).wait_send()

    for h in range(heads):
        for d in distances:
            to_x(d, h, 0).wait_send()
        for d in [0] + distances:
            across(d, h, 0).wait_send()


def solution(mesh):
    nh = mesh.shape["head"]
    nz = nh
    ny = mesh.shape["seq"] // nz
    nx = nh // 2

    def per_device(queries, key_vectors, values, strengths, out_weight):
        toks = queries.shape[0]
        heads = strengths.shape[1]
        dk = queries.shape[1] // heads
        cols = out_weight.shape[1]
        sl = dk // (ny // heads)
        vmem, dma = pltpu.VMEM, pltpu.SemaphoreType.DMA

        def ring(n):
            return [dma((2, n // 2, 2))] * 2

        return pl.pallas_call(
            functools.partial(kernel, nz, ny, nh),
            out_shape=jax.ShapeDtypeStruct((toks, ny * cols), BF16),
            in_specs=[pl.BlockSpec(memory_space=pl.ANY)] * 5,
            out_specs=pl.BlockSpec(memory_space=pltpu.VMEM),
            scratch_shapes=[
                vmem(queries.shape, BF16),
                vmem(key_vectors.shape, BF16),
                vmem(values.shape, BF16),
                vmem(strengths.shape, F32),
                vmem((cols, heads * dk), BF16),
                vmem((heads, 2 * toks, dk), F32),
                vmem((heads, 2 * toks, dk), F32),
                vmem((nz, ny, cols, dk), BF16),
                vmem((ny, nz, cols, dk), BF16),
                vmem((ny, dk + sl, dk), BF16),
                vmem((ny, dk + sl, dk), BF16),
                vmem((dk + sl, dk), BF16),
                vmem((nz, dk + sl, dk), BF16),
                vmem((dk, ny * dk), BF16),
                vmem((ny, sl, dk), F32),
                vmem((ny, sl, dk), BF16),
                vmem((ny, sl, dk), BF16),
                vmem((nh, heads, toks, dk), BF16),
                dma((5,)),
                dma((ny,)),
                dma((ny,)),
                dma((nz,)),
                dma((nh,)),
                *ring(nz),
                *ring(ny),
                dma((ny,)),
                dma((ny,)),
                dma((nz,)),
                dma((nz,)),
                dma((ny,)),
                dma((ny,)),
                dma((nx, heads)),
                dma((nx, heads)),
                dma((nx, heads)),
                dma((nx, heads)),
            ],
            compiler_params=pltpu.CompilerParams(
                collective_id=0, has_side_effects=True, vmem_limit_bytes=62 * 1024 * 1024
            ),
        )(queries, key_vectors, values, strengths, out_weight.T)

    return jax.shard_map(
        per_device,
        mesh=mesh,
        in_specs=(
            P("seq", "head"),
            P(None, "seq", "head"),
            P(None, "seq", "head"),
            P(None, "head", "seq"),
            P("head", "seq"),
        ),
        out_specs=P("seq", "head"),
        check_vma=False,
    )
```
